128 devices in a mesh: grp: 2 (over core), tp: 32 (over z, x_lo, y), dp: 2 (over x_hi).
Axes of the slice: x: 4 (x_hi: 2, x_lo: 2; x = x_hi * 2 + x_lo), y: 4, z: 4, core: 2. Of those that a mesh axis runs over, the one named last changes fastest.
Arguments:
- base_inputs: bfloat16 [3, 128, 8192], P(None, 'dp', ('grp', 'tp')), may hold values from -6 to 6
- small_inputs: bfloat16 [2, 3, 128, 4096], P('grp', None, 'dp', 'tp'), may hold values from -6 to 6
- base_norm_gain: float32 [8192], replicated, may hold values from 0.1 to 1.9
- base_query: bfloat16 [8192, 8192], P(None, ('grp', 'tp')), may hold values from -0.0625 to 0.0625
- base_keys_values: bfloat16 [2, 8192, 1024], P(None, None, ('grp', 'tp')), may hold values from -0.0625 to 0.0625
- base_output: bfloat16 [8192, 8192], P(('grp', 'tp')), may hold values from -0.0625 to 0.0625
- base_cache: bfloat16 [2, 128, 1024, 128], P(None, 'dp', ('grp', 'tp')), may hold values from -600 to 600
- base_final_gain: float32 [8192], replicated, may hold values from 0.1 to 1.9
- base_unembed: bfloat16 [16384, 8192], P(('grp', 'tp')), may hold values from -20 to 20
- small_norm_gain: float32 [2, 4096], P('grp'), may hold values from 0.1 to 1.9
- small_projections: bfloat16 [2, 3, 4096, 4096], P('grp', None, None, 'tp'), may hold values from -0.09375 to 0.09375
- small_output: bfloat16 [2, 4096, 4096], P('grp', 'tp'), may hold values from -0.09375 to 0.09375
- small_cache: bfloat16 [2, 2, 128, 4096, 128], P('grp', None, 'dp', 'tp'), may hold values from -600 to 600
- small_final_gain: float32 [2, 4096], P('grp'), may hold values from 0.1 to 1.9
- small_unembed: bfloat16 [2, 2, 8192, 4096], P('grp', None, 'tp'), may hold values from -0.1875 to 0.1875
- lengths: int32 [128], P('dp'), may hold values from 1 to 128, as said below
- next_tokens: int32 [3, 128], P(None, 'dp'), may hold values from 0 to 16383
Outputs:
- log_probs: float32 [3, 128, 16384], P(None, 'dp', ('grp', 'tp'))
- chosen_total: float32 [128], P('dp')
The draws below stay inside these ranges and needn't reach their ends.
Inputs may be any that keep to these rules, and one draw needn't show every extreme that they name: `lengths`: some row holds 128 cached positions.
All inputs are finite; a program needn't handle non-finite values.
Results may differ from the reference program's by a relative error of at most 0.0035.
Values may be sent and summed in bfloat16 or wider, within the bound.
No kernel may reach another device: no remote copies, remote signals or barrier semaphores. Data moves between devices by JAX's collectives and lax.ppermute only.
A program may use at most 128 MiB of HBM per device.

```python
import math
import jax
import jax.numpy as jnp
from jax import lax

DB = 8192
HB = 64
KVB = 8
HD = 128
DS = 4096
HS = 32
VOCAB = 16384
STEPS = 3
CACHE = 128
ROWS = 128
N_GRP = 2
N_TP = 32


def cache_draw(key, full_shape):
    key_entries = jax.random.fold_in(key, 0)
    entries = jnp.clip(jax.random.normal(key_entries, full_shape, jnp.float32), -6.0, 6.0)
    key_factor = jnp.ones((ROWS, 1, CACHE), jnp.float32)
    factor = jnp.stack([key_factor, jnp.full((ROWS, 1, CACHE), 3.0, jnp.float32)], axis=0)
    return (entries * factor).astype(jnp.bfloat16)


def draw_base_cache(key, part):
    return cache_draw(key, (2, ROWS, KVB * HD, CACHE))


def draw_small_cache(key, part):
    return cache_draw(key, (2, 2, ROWS, HS * HD, CACHE))


def draw_base_unembed(key, part):
    key_entries = jax.random.fold_in(key, 0)
    spread = 3.0 / math.sqrt(DB)
    entries = jnp.clip(jax.random.normal(key_entries, (VOCAB, DB), jnp.float32), -6.0, 6.0) * spread
    return entries.astype(jnp.bfloat16)


def draw_lengths(key, part):
    key_values, key_spot = jax.random.split(key, 2)
    drawn = jax.random.randint(key_values, (ROWS,), 1, CACHE + 1)
    longest = jax.random.randint(key_spot, (), 0, ROWS)
    return jnp.where(jnp.arange(ROWS) == longest, CACHE, drawn).astype(jnp.int32)


def place_ends(result, rng, least, largest):
    extent = result.shape
    place = [jax.random.randint(jax.random.fold_in(rng, axis), (), 0, extent[axis]) for axis in range(len(extent))]
    result = result.at[tuple(place)].set(least)
    longest = extent.index(max(extent))
    place[longest] = (place[longest] + 1) % extent[longest]
    return result.at[tuple(place)].set(largest)


def block_levels(key, extent, pieces, least, high):
    gain = 1.0
    for dim, parts in pieces:
        draws = jax.random.uniform(jax.random.fold_in(jax.random.fold_in(key, 6), dim), (parts,), jnp.float32, least / len(pieces), high / len(pieces))
        gain = gain * jnp.repeat(jnp.exp(draws), extent[dim] // parts).reshape((-1,) + (1,) * (len(extent) - 1 - dim))
    return gain


def centred(stream_key, dims, scale, most, cuts=(), kind=jnp.bfloat16):
    values = scale * jax.random.normal(stream_key, dims, jnp.float32)
    if cuts:
        values = values * block_levels(stream_key, dims, cuts, -0.22, 0.18)
    return jnp.clip(values, -most, most).astype(kind)


def setup_inputs(seed: int = 0) -> dict:
    arg_keys = jax.random.split(jax.random.key(seed), 18)
    base_inputs = centred(arg_keys[0], (STEPS, ROWS, DB), 1.0, 6.0, ((1, 2), (2, 64)))
    small_inputs = centred(arg_keys[1], (2, STEPS, ROWS, DS), 1.0, 6.0, ((0, 2), (2, 2), (3, 32)))
    base_norm_gain = jnp.clip(1.0 + 0.18 * jax.random.normal(arg_keys[2], (DB,), jnp.float32), 0.1, 1.9)
    base_query = centred(arg_keys[3], (DB, HB * HD), DB ** -0.5, 0.0625, ((1, 64),))
    base_keys_values = centred(arg_keys[4], (2, DB, KVB * HD), DB ** -0.5, 0.0625, ((2, 64),))
    base_output = centred(arg_keys[5], (HB * HD, DB), (HB * HD) ** -0.5, 0.0625, ((0, 64),))
    base_cache = draw_base_cache(jax.random.fold_in(arg_keys[17], 71), 0)
    base_final_gain = jnp.clip(1.0 + 0.18 * jax.random.normal(arg_keys[7], (DB,), jnp.float32), 0.1, 1.9)
    base_unembed = draw_base_unembed(jax.random.fold_in(arg_keys[17], 71), 0)
    small_norm_gain = jnp.clip(1.0 + 0.18 * jax.random.normal(arg_keys[9], (2, DS), jnp.float32), 0.1, 1.9)
    small_projections = centred(arg_keys[10], (2, 3, DS, HS * HD), DS ** -0.5, 0.09375, ((0, 2), (3, 32)))
    small_output = centred(arg_keys[11], (2, HS * HD, DS), (HS * HD) ** -0.5, 0.09375, ((0, 2), (1, 32)))
    small_cache = draw_small_cache(jax.random.fold_in(arg_keys[17], 71), 0)
    small_final_gain = jnp.clip(1.0 + 0.18 * jax.random.normal(arg_keys[13], (2, DS), jnp.float32), 0.1, 1.9)
    small_unembed = centred(arg_keys[14], (2, 2, VOCAB // 2, DS), (DS // 4) ** -0.5, 0.1875, ((0, 2), (2, 32)))
    lengths = draw_lengths(jax.random.fold_in(arg_keys[17], 71), 0)
    next_tokens = place_ends(jax.random.randint(arg_keys[16], (STEPS, ROWS), 0, VOCAB), jax.random.fold_in(arg_keys[16], 1), 0, VOCAB - 1).astype(jnp.int32)
    return dict(base_inputs=base_inputs, small_inputs=small_inputs, base_norm_gain=base_norm_gain, base_query=base_query, base_keys_values=base_keys_values, base_output=base_output, base_cache=base_cache, base_final_gain=base_final_gain, base_unembed=base_unembed, small_norm_gain=small_norm_gain, small_projections=small_projections, small_output=small_output, small_cache=small_cache, small_final_gain=small_final_gain, small_unembed=small_unembed, lengths=lengths, next_tokens=next_tokens)


EPSILON = 1e-05
NEGATIVE = -1e+30

def rotate_pairs(values, positions, first_pair, head_size):
    pair_count = values.shape[-1] // 2
    pair_index = (first_pair + jnp.arange(pair_count)).astype(jnp.float32)
    frequency = jnp.exp(pair_index * (-2.0 * math.log(10000.0) / head_size))
    angles = positions.astype(jnp.float32)[:, None] * frequency[None, :]
    angles = angles.reshape((values.shape[0],) + (1,) * (values.ndim - 2) + (pair_count,))
    cosine = jnp.cos(angles)
    sine_part = jnp.sin(angles)
    paired = values.reshape(values.shape[:-1] + (pair_count, 2))
    even_part = paired[..., 0]
    odd_part = paired[..., 1]
    turned = jnp.stack([even_part * cosine - odd_part * sine_part, even_part * sine_part + odd_part * cosine], axis=-1)
    return turned.reshape(values.shape)

def norm_rows(values, gain_row):
    values = values.astype(jnp.float32)
    scaling = lax.rsqrt(lax.optimization_barrier(jnp.mean(values * values, axis=-1, keepdims=True)) + EPSILON)
    return (values * scaling * gain_row).astype(jnp.bfloat16)

def attention_weights(cached_scores, fresh_scores, visible, head_size):
    factor = 1.0 / math.sqrt(head_size)
    cached_scores = jnp.where(visible, cached_scores * factor, NEGATIVE)
    fresh_scores = fresh_scores * factor
    row_max = jnp.maximum(lax.optimization_barrier(jnp.max(cached_scores, axis=-1, keepdims=True)), lax.optimization_barrier(jnp.max(fresh_scores, axis=-1, keepdims=True)))
    cached_exp = jnp.exp(cached_scores - row_max)
    fresh_exp = jnp.exp(fresh_scores - row_max)
    totals = lax.optimization_barrier(jnp.sum(cached_exp, axis=-1, keepdims=True)) + lax.optimization_barrier(jnp.sum(fresh_exp, axis=-1, keepdims=True))
    return ((cached_exp / totals).astype(jnp.bfloat16), (fresh_exp / totals).astype(jnp.bfloat16))

def small_model(model_index, small_inputs, lengths, small_norm_gain, small_projections, small_output, small_cache, small_final_gain, small_unembed):
    visible = (jnp.arange(CACHE)[None, :] < lengths[:, None])[:, None, :]
    keys_cached = small_cache[model_index, 0].reshape(ROWS, HS, HD, CACHE).astype(jnp.float32)
    values_cached = small_cache[model_index, 1].reshape(ROWS, HS, HD, CACHE).astype(jnp.float32)
    vocab_table = small_unembed[model_index].reshape(VOCAB, DS)
    new_keys = []
    new_values = []
    logit_steps = []
    for step_index in range(STEPS):
        positions = lengths + step_index
        inputs_now = small_inputs[model_index, step_index]
        normed = norm_rows(inputs_now, small_norm_gain[model_index])
        queries = jnp.dot(normed, small_projections[model_index, 0], preferred_element_type=jnp.float32).reshape(ROWS, HS, HD)
        queries = rotate_pairs(queries, positions, 0, HD).astype(jnp.bfloat16)
        new_key = jnp.dot(normed, small_projections[model_index, 1], preferred_element_type=jnp.float32).reshape(ROWS, HS, HD)
        new_keys.append(rotate_pairs(new_key, positions, 0, HD).astype(jnp.bfloat16))
        new_value = jnp.dot(normed, small_projections[model_index, 2], preferred_element_type=jnp.float32).reshape(ROWS, HS, HD)
        new_values.append(new_value.astype(jnp.bfloat16))
        fresh_keys = jnp.stack(new_keys, axis=-1).astype(jnp.float32)
        fresh_values = jnp.stack(new_values, axis=-1).astype(jnp.float32)
        queries_wide = queries.astype(jnp.float32)
        cached_scores = jnp.einsum('rhd,rhdl->rhl', queries_wide, keys_cached)
        fresh_scores = jnp.einsum('rhd,rhdn->rhn', queries_wide, fresh_keys)
        cached_weights, fresh_weights = attention_weights(cached_scores, fresh_scores, visible, HD)
        head_values = jnp.einsum('rhl,rhdl->rhd', cached_weights.astype(jnp.float32), values_cached)
        head_values = head_values + jnp.einsum('rhn,rhdn->rhd', fresh_weights.astype(jnp.float32), fresh_values)
        head_values = head_values.astype(jnp.bfloat16).reshape(ROWS, HS * HD)
        hidden = inputs_now.astype(jnp.float32) + jnp.dot(head_values, small_output[model_index], preferred_element_type=jnp.float32)
        final_rows = norm_rows(hidden, small_final_gain[model_index])
        logit_steps.append(jnp.dot(final_rows, vocab_table.T, preferred_element_type=jnp.float32))
    return logit_steps

def base_model(base_inputs, lengths, base_norm_gain, base_query, base_keys_values, base_output, base_cache, base_final_gain, base_unembed):
    share_count = N_GRP * N_TP // KVB
    slice_width = HD // share_count
    group_size = HB // KVB
    visible = (jnp.arange(CACHE)[None, :] < lengths[:, None])[:, None, None, :]
    keys_cached = base_cache[0].reshape(ROWS, KVB, HD, CACHE).astype(jnp.float32)
    values_cached = base_cache[1].reshape(ROWS, KVB, HD, CACHE).astype(jnp.float32)
    new_keys = []
    new_values = []
    logit_steps = []
    for step_index in range(STEPS):
        positions = lengths + step_index
        inputs_now = base_inputs[step_index]
        normed = norm_rows(inputs_now, base_norm_gain)
        queries = jnp.dot(normed, base_query, preferred_element_type=jnp.float32)
        queries = queries.reshape(ROWS, KVB, share_count, group_size, slice_width).transpose(0, 1, 3, 2, 4).reshape(ROWS, KVB, group_size, HD)
        queries = rotate_pairs(queries, positions, 0, HD).astype(jnp.bfloat16)
        new_key = jnp.dot(normed, base_keys_values[0], preferred_element_type=jnp.float32).reshape(ROWS, KVB, HD)
        new_keys.append(rotate_pairs(new_key, positions, 0, HD).astype(jnp.bfloat16))
        new_value = jnp.dot(normed, base_keys_values[1], preferred_element_type=jnp.float32).reshape(ROWS, KVB, HD)
        new_values.append(new_value.astype(jnp.bfloat16))
        fresh_keys = jnp.stack(new_keys, axis=-1).astype(jnp.float32)
        fresh_values = jnp.stack(new_values, axis=-1).astype(jnp.float32)
        queries_wide = queries.astype(jnp.float32)
        cached_scores = jnp.einsum('rkgd,rkdl->rkgl', queries_wide, keys_cached)
        fresh_scores = jnp.einsum('rkgd,rkdn->rkgn', queries_wide, fresh_keys)
        cached_weights, fresh_weights = attention_weights(cached_scores, fresh_scores, visible, HD)
        head_values = jnp.einsum('rkgl,rkdl->rkgd', cached_weights.astype(jnp.float32), values_cached)
        head_values = head_values + jnp.einsum('rkgn,rkdn->rkgd', fresh_weights.astype(jnp.float32), fresh_values)
        head_values = head_values.astype(jnp.bfloat16).reshape(ROWS, KVB, group_size, share_count, slice_width)
        head_values = head_values.transpose(0, 1, 3, 2, 4).reshape(ROWS, HB * HD)
        hidden = inputs_now.astype(jnp.float32) + jnp.dot(head_values, base_output, preferred_element_type=jnp.float32)
        final_rows = norm_rows(hidden, base_final_gain)
        logit_steps.append(jnp.dot(final_rows, base_unembed.T, preferred_element_type=jnp.float32))
    return logit_steps

def reference(base_inputs, small_inputs, base_norm_gain, base_query, base_keys_values, base_output, base_cache, base_final_gain, base_unembed, small_norm_gain, small_projections, small_output, small_cache, small_final_gain, small_unembed, lengths, next_tokens):
    expert_steps = small_model(0, small_inputs, lengths, small_norm_gain, small_projections, small_output, small_cache, small_final_gain, small_unembed)
    anti_steps = small_model(1, small_inputs, lengths, small_norm_gain, small_projections, small_output, small_cache, small_final_gain, small_unembed)
    base_steps = base_model(base_inputs, lengths, base_norm_gain, base_query, base_keys_values, base_output, base_cache, base_final_gain, base_unembed)
    log_steps = []
    chosen_total = jnp.zeros((ROWS,), jnp.float32)
    for step_index in range(STEPS):
        steered = base_steps[step_index] + expert_steps[step_index] - anti_steps[step_index]
        row_max = lax.optimization_barrier(jnp.max(steered, axis=-1, keepdims=True))
        log_norm = row_max + jnp.log(lax.optimization_barrier(jnp.sum(jnp.exp(steered - row_max), axis=-1, keepdims=True)))
        step_probs = steered - log_norm
        log_steps.append(step_probs)
        chosen_total = chosen_total + jnp.take_along_axis(step_probs, next_tokens[step_index][:, None].astype(jnp.int32), axis=1)[:, 0]
    return (jnp.stack(log_steps, axis=0), chosen_total)
```

```python
import math

import jax
import jax.numpy as jnp
from jax import lax
from jax.sharding import Mesh, PartitionSpec as P

HD = 128
STEPS = 3
CACHE = 128
EPSILON = 1e-05
NEGATIVE = -1e30
CHIPS = ("z", "xl", "y")
EVERY = ("grp",) + CHIPS
PLANE = ("xl", "y")
F32 = jnp.float32
BF16 = jnp.bfloat16


def gather_chips(shard):
    count = lax.axis_size(CHIPS)
    copies = jnp.broadcast_to(shard[None], (count,) + shard.shape)
    return lax.all_to_all(copies, CHIPS, 0, 0, tiled=True)


def scatter_chips(blocks):
    received = lax.all_to_all(blocks, CHIPS, 0, 0, tiled=True)
    return jnp.sum(received.astype(F32), axis=0)


def swap_cores(array):
    return lax.ppermute(array, "grp", [(0, 1), (1, 0)])


def rotation(positions, first_pair, pair_count):
    pair_index = (first_pair + jnp.arange(pair_count)).astype(F32)
    frequency = jnp.exp(pair_index * (-2.0 * math.log(10000.0) / HD))
    angles = positions.astype(F32)[..., None] * frequency
    return jnp.cos(angles), jnp.sin(angles)


def rotate_pairs(values, cosine, sine):
    paired = values.reshape(values.shape[:-1] + (-1, 2))
    even, odd = paired[..., 0], paired[..., 1]
    turned = jnp.stack([even * cosine - odd * sine, even * sine + odd * cosine], axis=-1)
    return turned.reshape(values.shape)


def attend(queries, keys, values, fresh_keys, fresh_values, lengths):
    rows, steps, group, size = queries.shape
    factor = 1.0 / math.sqrt(HD)
    flat = queries.reshape(rows, steps * group, size)
    cached = jnp.einsum("rqd,rdl->rql", flat, keys, preferred_element_type=F32)
    fresh = jnp.einsum("rqd,rnd->rqn", flat, fresh_keys, preferred_element_type=F32)
    visible = (jnp.arange(CACHE)[None, :] < lengths[:, None])[:, None, :]
    step_of = jnp.arange(steps * group) // group
    seen = (jnp.arange(steps)[None, :] <= step_of[:, None])[None]
    cached = jnp.where(visible, cached * factor, NEGATIVE)
    fresh = jnp.where(seen, fresh * factor, NEGATIVE)
    top = jnp.maximum(jnp.max(cached, -1, keepdims=True), jnp.max(fresh, -1, keepdims=True))
    cached = jnp.exp(cached - top)
    fresh = jnp.exp(fresh - top)
    total = jnp.sum(cached, -1, keepdims=True) + jnp.sum(fresh, -1, keepdims=True)
    cached = (cached / total).astype(BF16)
    fresh = (fresh / total).astype(BF16)
    out = jnp.einsum("rql,rdl->rqd", cached, values, preferred_element_type=F32)
    out = out + jnp.einsum("rqn,rnd->rqd", fresh, fresh_values, preferred_element_type=F32)
    return out.astype(BF16).reshape(rows, steps, group, size)


def norm_rows(values, gain_row):
    values = values.astype(F32)
    scaling = lax.rsqrt(jnp.mean(values * values, axis=-1, keepdims=True) + EPSILON)
    return (values * scaling * gain_row).astype(BF16)


def body(
    base_inputs,
    small_inputs,
    base_norm_gain,
    base_query,
    base_keys_values,
    base_output,
    base_cache,
    base_final_gain,
    base_unembed,
    small_norm_gain,
    small_projections,
    small_output,
    small_cache,
    small_final_gain,
    small_unembed,
    lengths,
    next_tokens,
):
    rows = lengths.shape[0]
    every_row = STEPS * rows
    chips = lax.axis_size(CHIPS)
    shares = lax.axis_size(PLANE)
    core = lax.axis_index("grp")
    chip = lax.axis_index(CHIPS)
    block = core * chips + chip
    share = lax.axis_index(PLANE)
    width = base_inputs.shape[2]
    slice_width = base_keys_values.shape[2]
    group = base_query.shape[1] // slice_width
    part_rows = rows // shares
    vocab_width = base_unembed.shape[0]
    positions = lengths[None, :] + jnp.arange(STEPS)[:, None]

    def both_halves(mine):
        other = swap_cores(mine)
        return jnp.where(
            core == 0, jnp.concatenate([mine, other]), jnp.concatenate([other, mine])
        )

    def whole_rows(blocks):
        return blocks.transpose(1, 0, 2).reshape(every_row, -1)

    cache = base_cache.reshape(2, shares, part_rows, slice_width, CACHE).transpose(1, 0, 2, 3, 4)
    cache = lax.all_to_all(cache, PLANE, 0, 0, tiled=True)
    cache = cache.transpose(1, 2, 0, 3, 4).reshape(2, part_rows, HD, CACHE)

    base_in = base_inputs.reshape(every_row, width)
    small_in = small_inputs[0].reshape(every_row, width)
    inputs = gather_chips(jnp.stack([base_in, small_in]))
    base_full = whole_rows(both_halves(inputs[:, 0]))
    small_full = whole_rows(inputs[:, 1])

    base_normed = norm_rows(base_full, base_norm_gain)
    queries = jnp.dot(base_normed, base_query, preferred_element_type=F32)
    keys = jnp.dot(base_normed, base_keys_values[0], preferred_element_type=F32)
    values = jnp.dot(base_normed, base_keys_values[1], preferred_element_type=F32)
    cosine, sine = rotation(positions, share * (slice_width // 2), slice_width // 2)
    queries = rotate_pairs(
        queries.reshape(STEPS, rows, group, slice_width), cosine[:, :, None], sine[:, :, None]
    )
    keys = rotate_pairs(keys.reshape(STEPS, rows, slice_width), cosine, sine)
    packed = jnp.concatenate(
        [
            queries.reshape(STEPS, rows, group * slice_width),
            keys,
            values.reshape(STEPS, rows, slice_width),
        ],
        axis=-1,
    ).astype(BF16)
    packed = packed.reshape(STEPS, shares, part_rows, -1).transpose(1, 0, 2, 3)
    packed = lax.all_to_all(packed, PLANE, 0, 0, tiled=True)
    wide = group * slice_width
    queries = packed[..., :wide].reshape(shares, STEPS, part_rows, group, slice_width)
    queries = queries.transpose(2, 1, 3, 0, 4).reshape(part_rows, STEPS, group, HD)
    keys = packed[..., wide : wide + slice_width].transpose(2, 1, 0, 3)
    values = packed[..., wide + slice_width :].transpose(2, 1, 0, 3)
    part_lengths = lax.dynamic_slice_in_dim(lengths, share * part_rows, part_rows)
    heads = attend(
        queries,
        cache[0],
        cache[1],
        keys.reshape(part_rows, STEPS, HD),
        values.reshape(part_rows, STEPS, HD),
        part_lengths,
    )
    heads = heads.reshape(part_rows, STEPS, group, shares, slice_width).transpose(3, 1, 0, 2, 4)
    heads = lax.all_to_all(
        heads.reshape(shares, STEPS, part_rows, wide), PLANE, 0, 0, tiled=True
    )
    heads = heads.transpose(1, 0, 2, 3).reshape(every_row, wide)

    small_normed = norm_rows(small_full, small_norm_gain[0])
    cosine, sine = rotation(positions, 0, HD // 2)
    small_q, small_k, small_v = (
        jnp.dot(small_normed, small_projections[0, i], preferred_element_type=F32).reshape(
            STEPS, rows, HD
        )
        for i in range(3)
    )
    small_q = rotate_pairs(small_q, cosine, sine).astype(BF16).transpose(1, 0, 2)
    small_k = rotate_pairs(small_k, cosine, sine).astype(BF16).transpose(1, 0, 2)
    small_v = small_v.astype(BF16).transpose(1, 0, 2)
    small_heads = attend(
        small_q[:, :, None], small_cache[0, 0], small_cache[0, 1], small_k, small_v, lengths
    )
    small_heads = small_heads.transpose(1, 0, 2, 3).reshape(every_row, HD)

    def chip_blocks(array):
        return array.reshape(every_row, chips, width).transpose(1, 0, 2)

    base_mixed = jnp.dot(heads, base_output, preferred_element_type=F32)
    half = base_mixed.shape[1] // 2
    first, second = base_mixed[:, :half], base_mixed[:, half:]
    kept = jnp.where(core == 0, first, second)
    other = swap_cores(jnp.where(core == 0, second, first).astype(BF16))
    base_mixed = (kept + other.astype(F32)).astype(BF16)
    small_mixed = jnp.dot(small_heads, small_output[0], preferred_element_type=F32).astype(BF16)
    sums = scatter_chips(
        jnp.stack([chip_blocks(base_mixed), chip_blocks(small_mixed)], axis=1)
    )
    base_hidden = base_in.astype(F32) + sums[0]
    small_hidden = small_in.astype(F32) + sums[1]

    base_gain = lax.dynamic_slice_in_dim(base_final_gain, block * width, width)
    small_gain = lax.dynamic_slice_in_dim(small_final_gain[0], chip * width, width)
    finals = gather_chips(
        jnp.stack([base_hidden * base_gain, small_hidden * small_gain]).astype(BF16)
    )
    base_final = whole_rows(both_halves(finals[:, 0]))
    small_final = whole_rows(finals[:, 1])

    def row_scale(gained, gain):
        plain = gained.astype(F32) * (1.0 / gain)
        return lax.rsqrt(jnp.mean(plain * plain, axis=-1, keepdims=True) + EPSILON)

    across = (((1,), (1,)), ((), ()))
    base_logits = lax.dot_general(base_final, base_unembed, across, preferred_element_type=F32)
    base_logits = base_logits * row_scale(base_final, base_final_gain)
    table = small_unembed[0].reshape(-1, small_unembed.shape[3])
    small_logits = lax.dot_general(small_final, table, across, preferred_element_type=F32)
    small_logits = small_logits * row_scale(small_final, small_final_gain[0])
    low, high = small_logits[:, :vocab_width], small_logits[:, vocab_width:]
    theirs = swap_cores(jnp.where(core == 0, high, low))
    ours = jnp.where(core == 0, low, high)
    steered = base_logits + jnp.where(core == 0, ours - theirs, theirs - ours)

    local_max = jnp.max(steered, axis=-1)
    local_sum = jnp.sum(jnp.exp(steered - local_max[:, None]), axis=-1)
    local_token = next_tokens.reshape(every_row) - block * vocab_width
    hit = jnp.arange(vocab_width)[None, :] == local_token[:, None]
    picked = jnp.sum(jnp.where(hit, steered, 0.0), axis=-1)
    triple = jnp.stack([local_max, local_sum, picked])
    count = lax.axis_size(EVERY)
    triples = lax.all_to_all(
        jnp.broadcast_to(triple[None], (count,) + triple.shape), EVERY, 0, 0, tiled=True
    )
    top = jnp.max(triples[:, 0], axis=0)
    total = jnp.sum(triples[:, 1] * jnp.exp(triples[:, 0] - top[None]), axis=0)
    log_norm = top + jnp.log(total)
    chosen = jnp.sum(triples[:, 2], axis=0) - log_norm
    log_probs = (steered - log_norm[:, None]).reshape(STEPS, rows, vocab_width)
    return log_probs, jnp.sum(chosen.reshape(STEPS, rows), axis=0)


def solution(mesh):
    devices = mesh.devices
    fine = Mesh(devices.reshape(2, 4, 2, 4, 2), ("grp", "z", "xl", "y", "dp"))
    placed = (
        P(None, "dp", EVERY),
        P("grp", None, "dp", CHIPS),
        P(),
        P(None, EVERY),
        P(None, None, EVERY),
        P(EVERY, None),
        P(None, "dp", EVERY, None),
        P(),
        P(EVERY, None),
        P("grp", None),
        P("grp", None, None, CHIPS),
        P("grp", CHIPS, None),
        P("grp", None, "dp", CHIPS, None),
        P("grp", None),
        P("grp", None, CHIPS, None),
        P("dp"),
        P(None, "dp"),
    )
    return jax.shard_map(
        body,
        mesh=fine,
        in_specs=placed,
        out_specs=(P(None, "dp", EVERY), P("dp")),
        check_vma=False,
    )
```

```python
import math

import jax
import jax.numpy as jnp
from jax import lax
from jax.experimental import pallas as pl
from jax.experimental.pallas import tpu as pltpu
from jax.sharding import Mesh, PartitionSpec as P

HD = 128
STEPS = 3
CACHE = 128
EPSILON = 1e-05
NEGATIVE = -1e30
CHIPS = ("z", "xl", "y")
EVERY = ("grp",) + CHIPS
PLANE = ("xl", "y")
F32 = jnp.float32
BF16 = jnp.bfloat16


RING = (0, -1, 1, 2)


def hop(array, across, first, second):
    sizes = [lax.axis_size(name) for name in EVERY]

    def index(*place):
        total = 0
        for at, size in zip(place, sizes):
            total = total * size + at % size
        return total

    pairs = []
    for core in range(sizes[0]):
        dz, dy = (second, first) if core == 0 else (first, second)
        for z in range(sizes[1]):
            for x in range(sizes[2]):
                for y in range(sizes[3]):
                    pairs.append(
                        (index(core, z, x, y), index(core, z + dz, x + across, y + dy))
                    )
    return lax.ppermute(array, EVERY, pairs)


def chip_order():
    z, x, y = (lax.axis_index(name) for name in CHIPS)
    sizes = [lax.axis_size(name) for name in CHIPS]
    core = lax.axis_index("grp")
    ring = jnp.array(RING, jnp.int32)
    second, first, flip = ring[:, None, None], ring[None, :, None], jnp.arange(2)[None, None, :]
    dz = jnp.where(core == 0, second, first)
    dy = jnp.where(core == 0, first, second)
    place = ((z + dz) % sizes[0] * sizes[1] + (x + flip) % sizes[1]) * sizes[2]
    return (place + (y + dy) % sizes[2]).reshape(-1).astype(jnp.int32)


def gather_chips(shard):
    two = jnp.stack([shard, hop(shard, 1, 0, 0)])
    eight = jnp.concatenate([two] + [hop(two, 0, -d, 0) for d in RING[1:]])
    return [eight] + [hop(eight, 0, 0, -d) for d in RING[1:]]


def scatter_chips(pieces):
    def total(own, others):
        result = own.astype(F32)
        for other in others:
            result = result + other.astype(F32)
        return result

    eight = total(pieces[0], [hop(p, 0, 0, d) for p, d in zip(pieces[1:], RING[1:])])
    sent = eight[2:].astype(BF16)
    two = total(
        eight[:2], [hop(sent[2 * i : 2 * i + 2], 0, d, 0) for i, d in enumerate(RING[1:])]
    )
    return two[0] + hop(two[1].astype(BF16), 1, 0, 0).astype(F32)


def swap_cores(array):
    return lax.ppermute(array, "grp", [(0, 1), (1, 0)])


def rotation(positions, first_pair, pair_count):
    pair_index = (first_pair + jnp.arange(pair_count)).astype(F32)
    frequency = jnp.exp(pair_index * (-2.0 * math.log(10000.0) / HD))
    angles = positions.astype(F32)[..., None] * frequency
    return jnp.cos(angles), jnp.sin(angles)


def attend(queries, keys, values, fresh_keys, fresh_values, lengths):
    rows, steps, group, size = queries.shape
    factor = 1.0 / math.sqrt(HD)
    flat = queries.reshape(rows, steps * group, size)
    cached = jnp.einsum("rqd,rdl->rql", flat, keys, preferred_element_type=F32)
    fresh = jnp.einsum("rqd,rnd->rqn", flat, fresh_keys, preferred_element_type=F32)
    visible = (jnp.arange(CACHE)[None, :] < lengths[:, None])[:, None, :]
    step_of = jnp.arange(steps * group) // group
    seen = (jnp.arange(steps)[None, :] <= step_of[:, None])[None]
    cached = jnp.where(visible, cached * factor, NEGATIVE)
    fresh = jnp.where(seen, fresh * factor, NEGATIVE)
    top = jnp.maximum(jnp.max(cached, -1, keepdims=True), jnp.max(fresh, -1, keepdims=True))
    cached = jnp.exp(cached - top)
    fresh = jnp.exp(fresh - top)
    total = jnp.sum(cached, -1, keepdims=True) + jnp.sum(fresh, -1, keepdims=True)
    cached = (cached / total).astype(BF16)
    fresh = (fresh / total).astype(BF16)
    out = jnp.einsum("rql,rdl->rqd", cached, values, preferred_element_type=F32)
    out = out + jnp.einsum("rqn,rnd->rqd", fresh, fresh_values, preferred_element_type=F32)
    return out.astype(BF16).reshape(rows, steps, group, size)


VMEM = pltpu.VMEM
ACROSS = (((1,), (1,)), ((), ()))


def call(kernel, out_shapes, scratch, scalars, *arrays):
    in_specs = [pl.BlockSpec(memory_space=pltpu.SMEM)] * len(scalars)
    in_specs += [pl.BlockSpec(memory_space=VMEM)] * len(arrays)
    many = isinstance(out_shapes, (list, tuple))
    out_specs = pl.BlockSpec(memory_space=VMEM)
    return pl.pallas_call(
        kernel,
        out_shape=out_shapes,
        in_specs=in_specs,
        out_specs=[out_specs] * len(out_shapes) if many else out_specs,
        scratch_shapes=scratch,
        compiler_params=pltpu.CompilerParams(vmem_limit_bytes=40 * 2**20),
    )(*scalars, *arrays)


def lay_out(pieces, table, offset, width, lay):
    total = jnp.zeros((pieces[0].shape[1], width), F32)
    start = 0
    for piece in pieces:

        def step(i, total, piece=piece, start=start):
            return total + lay(piece[i, :, offset : offset + width], table[start + i])

        total = lax.fori_loop(0, piece.shape[0], step, total)
        start += piece.shape[0]
    return jnp.sum(total, axis=1, keepdims=True)


def column(t, width):
    return pl.ds(pl.multiple_of(t * width, width), width)


def lay_gained(pieces, table, offset, gain, laid):
    width = gain.shape[2]

    def lay(block, t):
        values = block.astype(F32)
        laid[:, column(t, width)] = (values * gain[t]).astype(BF16)
        return values * values

    return lay_out(pieces, table, offset, width, lay)


def lay_final(pieces, table, offset, inverse, laid):
    width = inverse.shape[2]

    def lay(block, t):
        laid[:, column(t, width)] = block
        values = block.astype(F32) * inverse[t]
        return values * values

    return lay_out(pieces, table, offset, width, lay)


def swap_pairs(values):
    lanes = values.shape[1]
    lane = lax.broadcasted_iota(jnp.int32, values.shape, 1)
    after = pltpu.roll(values, lanes - 1, 1)
    before = pltpu.roll(values, 1, 1)
    return jnp.where(lane % 2 == 0, after, before)


def project_base(pieces, table, core, gain, query, query_other, kv, kv_other):
    rows = pieces[0].shape[1]
    half = query_other.shape[0]
    wide = query.shape[1]
    slim = kv.shape[0]

    def kernel(table, core, *refs):
        parts = refs[: len(pieces)]
        gain, query, query_other, kv, kv_other, mine, theirs, laid, slot = refs[len(pieces) :]
        squares = lay_gained(parts, table, 0, gain, laid)
        values = laid[...]
        start = pl.multiple_of(core[0] * half, half)
        slot[...] = jnp.zeros_like(slot)
        lane = lax.broadcasted_iota(jnp.int32, slot.shape, 1)
        mine[:, :wide] = jnp.dot(
            values, query[pl.ds(start, half), :], preferred_element_type=F32
        )
        theirs[:, :wide] = jnp.dot(values, query_other[...], preferred_element_type=F32)
        slot[:, :slim] = lax.dot_general(
            values, kv[:, pl.ds(start, half)], ACROSS, preferred_element_type=F32
        )
        mine[:, wide:] = jnp.where(lane < slim, slot[...], squares)
        slot[:, :slim] = lax.dot_general(
            values, kv_other[...], ACROSS, preferred_element_type=F32
        )
        theirs[:, wide:] = jnp.where(lane < slim, slot[...], squares)

    shape = jax.ShapeDtypeStruct((rows, 2 * wide), F32)
    scratch = [VMEM((rows, half), BF16), VMEM((rows, wide), F32)]
    return call(
        kernel, [shape, shape], scratch, [table, core],
        *pieces, gain, query, query_other, kv, kv_other,
    )


def finish_base(mine, theirs, cosine, sine, features, slice_width):
    rows, lanes = mine.shape
    wide = lanes // 2

    def kernel(mine, theirs, cosine, sine, out):
        values = mine[...] + theirs[...]
        squares = values[:, lanes - 1 : lanes]
        scaling = lax.rsqrt(squares * (1.0 / features) + EPSILON)
        turned = scaling * (values * cosine[...] + swap_pairs(values) * sine[...])
        turned = turned.astype(BF16)
        source = lax.broadcasted_iota(jnp.int32, (wide, 2 * wide), 0)
        lane = lax.broadcasted_iota(jnp.int32, (wide, 2 * wide), 1)
        wanted = lane % slice_width + jnp.where(lane < wide, 0, slice_width)
        repeat = jnp.where(source == wanted, 1.0, 0.0).astype(BF16)
        out[:, :wide] = turned[:, :wide]
        out[:, wide:] = jnp.dot(
            turned[:, wide:], repeat, preferred_element_type=F32
        ).astype(BF16)

    shape = jax.ShapeDtypeStruct((rows, 3 * wide), BF16)
    return call(kernel, shape, [], [], mine, theirs, cosine, sine)


def attend_base(packed, cache, lengths, slice_width):
    shares, lined, lanes = packed.shape
    wide = lanes // 3
    part_rows = cache.shape[2]
    group = wide // slice_width
    queries = STEPS * group
    factor = 1.0 / math.sqrt(HD)

    def kernel(lengths, packed, cache, out, slot):
        sub = lax.broadcasted_iota(jnp.int32, (group, shares * wide), 0)
        lane = lax.broadcasted_iota(jnp.int32, (group, shares * wide), 1)
        own = lane % wide // slice_width == sub
        place = lax.broadcasted_iota(jnp.int32, (queries, CACHE), 1)
        fresh_place = lax.broadcasted_iota(jnp.int32, (queries, 16), 1)
        step_of = lax.broadcasted_iota(jnp.int32, (queries, 16), 0) // group
        seen = (fresh_place <= step_of) & (fresh_place < STEPS)
        blocks = [packed[c].astype(F32) for c in range(shares)]
        empty = jnp.zeros((16 - STEPS, shares * wide), F32)

        def line(row, start):
            return jnp.concatenate(
                [block[row : row + 1, start : start + wide] for block in blocks], axis=1
            )

        for r in range(part_rows):
            lines = [s * part_rows + r for s in range(STEPS)]
            asked = jnp.concatenate(
                [jnp.where(own, line(i, 0), 0.0) for i in lines], axis=0
            ).astype(BF16)
            keys = jnp.concatenate([line(i, wide) for i in lines] + [empty], 0).astype(BF16)
            values = jnp.concatenate([line(i, 2 * wide) for i in lines] + [empty], 0).astype(BF16)
            kept_keys = jnp.concatenate(
                [cache[c, 0, r] for c in range(shares) for _ in range(group)], axis=0
            )
            kept_values = jnp.concatenate(
                [cache[c, 1, r] for c in range(shares) for _ in range(group)], axis=0
            )
            cached = jnp.dot(asked, kept_keys, preferred_element_type=F32) * factor
            fresh = lax.dot_general(asked, keys, ACROSS, preferred_element_type=F32) * factor
            cached = jnp.where(place < lengths[r], cached, NEGATIVE)
            fresh = jnp.where(seen, fresh, NEGATIVE)
            top = jnp.maximum(
                jnp.max(cached, axis=1, keepdims=True), jnp.max(fresh, axis=1, keepdims=True)
            )
            cached = jnp.exp(cached - top)
            fresh = jnp.exp(fresh - top)
            total = jnp.sum(cached, axis=1, keepdims=True) + jnp.sum(fresh, axis=1, keepdims=True)
            cached = (cached / total).astype(BF16)
            fresh = (fresh / total).astype(BF16)
            result = lax.dot_general(cached, kept_values, ACROSS, preferred_element_type=F32)
            result = result + jnp.dot(fresh, values, preferred_element_type=F32)
            for s in range(STEPS):
                part = jnp.where(own, result[s * group : (s + 1) * group], 0.0)
                part = jnp.sum(part, axis=0, keepdims=True)
                for c in range(shares):
                    slot[c, lines[s] : lines[s] + 1, :] = part[:, c * wide : (c + 1) * wide]
        out[...] = slot[...].astype(BF16)

    shape = jax.ShapeDtypeStruct((shares, lined, wide), BF16)
    return call(kernel, shape, [VMEM((shares, lined, wide), F32)], [lengths], packed, cache)


def project_small(pieces, table, gain, projections, cosine, sine):
    rows = pieces[0].shape[1]
    features = projections.shape[1]
    wide = projections.shape[2]

    def kernel(table, *refs):
        parts = refs[: len(pieces)]
        gain, projections, cosine, sine, out, laid = refs[len(pieces) :]
        squares = lay_gained(parts, table, gain.shape[2], gain, laid)
        scaling = lax.rsqrt(squares * (1.0 / features) + EPSILON)
        for i in range(3):
            values = jnp.dot(laid[...], projections[i], preferred_element_type=F32) * scaling
            if i < 2:
                values = values * cosine[...] + swap_pairs(values) * sine[...]
            out[i] = values.astype(BF16)

    shape = jax.ShapeDtypeStruct((3, rows, wide), BF16)
    return call(
        kernel, shape, [VMEM((rows, features), BF16)], [table],
        *pieces, gain, projections, cosine, sine,
    )


def mix(heads, heads_other, small_heads, table, core, output, output_other, small_output, width):
    rows = heads.shape[0]
    count = table.shape[0]
    pieces = len(RING)
    each = count // pieces

    def kernel(table, core, heads, heads_other, small_heads, output, output_other, small_output,
               *outs):
        both = jnp.concatenate([heads[...], heads_other[...]], axis=1)
        small = small_heads[...]
        for piece in (3, 1, 2, 0):
            for i in range(each):
                t = table[piece * each + i]
                weights = jnp.concatenate(
                    [output[:, column(core[0] * count + t, width)],
                     output_other[:, column(t, width)]],
                    axis=0,
                )
                outs[piece][i, :, :width] = jnp.dot(
                    both, weights, preferred_element_type=F32
                ).astype(BF16)
                outs[piece][i, :, width:] = jnp.dot(
                    small, small_output[:, column(t, width)], preferred_element_type=F32
                ).astype(BF16)

    shape = jax.ShapeDtypeStruct((each, rows, 2 * width), BF16)
    return call(
        kernel, [shape] * pieces, [], [table, core],
        heads, heads_other, small_heads, output, output_other, small_output,
    )


def unembed_base(pieces, table, core, inverse, unembed, unembed_other):
    rows = pieces[0].shape[1]
    vocab, half = unembed_other.shape

    def kernel(table, core, *refs):
        parts = refs[: len(pieces)]
        inverse, unembed, unembed_other, mine, theirs, squares, laid = refs[len(pieces) :]
        squares[...] = jnp.broadcast_to(lay_final(parts, table, 0, inverse, laid), squares.shape)
        start = pl.multiple_of(core[0] * half, half)
        mine[...] = lax.dot_general(
            laid[...], unembed[:, pl.ds(start, half)], ACROSS, preferred_element_type=F32
        )
        theirs[...] = lax.dot_general(
            laid[...], unembed_other[...], ACROSS, preferred_element_type=F32
        )

    shape = jax.ShapeDtypeStruct((rows, vocab), F32)
    return call(
        kernel, [shape, shape, jax.ShapeDtypeStruct((rows, 128), F32)],
        [VMEM((rows, half), BF16)], [table, core],
        *pieces, inverse, unembed, unembed_other,
    )


def unembed_small(pieces, table, core, inverse, unembed):
    rows = pieces[0].shape[1]
    vocab, features = unembed.shape

    def kernel(table, core, *refs):
        parts = refs[: len(pieces)]
        inverse, unembed, out, laid = refs[len(pieces) :]
        squares = lay_final(parts, table, inverse.shape[2], inverse, laid)
        scaling = lax.rsqrt(squares * (1.0 / features) + EPSILON)
        scaling = jnp.where(core[0] == 0, scaling, -scaling)
        out[...] = scaling * lax.dot_general(
            laid[...], unembed[...], ACROSS, preferred_element_type=F32
        )

    shape = jax.ShapeDtypeStruct((rows, vocab), F32)
    return call(
        kernel, shape, [VMEM((rows, features), BF16)], [table, core],
        *pieces, inverse, unembed,
    )


def body(
    base_inputs,
    small_inputs,
    base_norm_gain,
    base_query,
    base_keys_values,
    base_output,
    base_cache,
    base_final_gain,
    base_unembed,
    small_norm_gain,
    small_projections,
    small_output,
    small_cache,
    small_final_gain,
    small_unembed,
    lengths,
    next_tokens,
):
    rows = lengths.shape[0]
    every_row = STEPS * rows
    chips = lax.axis_size(CHIPS)
    shares = lax.axis_size(PLANE)
    core = lax.axis_index("grp")
    chip = lax.axis_index(CHIPS)
    block = core * chips + chip
    share = lax.axis_index(PLANE)
    width = base_inputs.shape[2]
    slice_width = base_keys_values.shape[2]
    wide = base_query.shape[1]
    group = wide // slice_width
    part_rows = rows // shares
    vocab_width = base_unembed.shape[0]
    features = base_query.shape[0]
    half = features // 2
    positions = lengths.reshape(shares, 1, part_rows) + jnp.arange(STEPS)[None, :, None]
    positions = positions.reshape(every_row)
    core_index = core.reshape(1).astype(jnp.int32)
    table = chip_order()

    def by_share(array):
        array = array.reshape((STEPS, shares, part_rows) + array.shape[2:])
        return array.swapaxes(0, 1).reshape((every_row,) + array.shape[3:])

    shard = jnp.concatenate([by_share(base_inputs), by_share(small_inputs[0])], axis=-1)
    inputs = gather_chips(shard)

    def send_half(array, axis):
        return swap_cores(lax.dynamic_slice_in_dim(array, (1 - core) * half, half, axis))

    kv = base_keys_values.transpose(0, 2, 1).reshape(2 * slice_width, features)
    query_other = send_half(base_query, 0)
    kv_other = send_half(kv, 1)
    output_other = send_half(base_output, 1)
    unembed_other = send_half(base_unembed, 1)

    cache = base_cache.reshape(2, shares, part_rows, slice_width, CACHE).transpose(1, 0, 2, 3, 4)
    cache, _ = lax.optimization_barrier((cache, inputs[0]))
    cache = lax.all_to_all(cache, PLANE, 0, 0, tiled=True)

    def by_chip(gain):
        return gain.reshape(chips, 1, width)

    def half_of(gain):
        return by_chip(lax.dynamic_slice_in_dim(gain, core * half, half))

    def turn(first_pair, pair_count, copies):
        cosine, sine = rotation(positions, first_pair, pair_count)
        cosine = jnp.repeat(cosine, 2, axis=-1)
        sine = jnp.stack([-sine, sine], axis=-1).reshape(cosine.shape)
        return jnp.tile(cosine, (1, copies)), jnp.tile(sine, (1, copies))

    cosine, sine = turn(share * (slice_width // 2), slice_width // 2, group + 1)
    ones = jnp.ones((every_row, slice_width), F32)
    rest = jnp.zeros((every_row, wide - 2 * slice_width), F32)
    cosine = jnp.concatenate([cosine, ones, rest], axis=-1)
    sine = jnp.concatenate([sine, 0.0 * ones, rest], axis=-1)

    mine, theirs = project_base(
        inputs, table, core_index, half_of(base_norm_gain),
        base_query, query_other, kv, kv_other,
    )
    packed = finish_base(mine, swap_cores(theirs), cosine, sine, features, slice_width)
    packed = packed.reshape(shares, STEPS * part_rows, 3 * wide)
    packed = lax.all_to_all(packed, PLANE, 0, 0, tiled=True)
    part_lengths = lax.dynamic_slice_in_dim(lengths, share * part_rows, part_rows)
    heads = attend_base(packed, cache, part_lengths, slice_width)
    heads = lax.all_to_all(heads, PLANE, 0, 0, tiled=True).reshape(every_row, wide)

    later, _ = lax.optimization_barrier((inputs, theirs))
    cosine, sine = turn(0, HD // 2, 1)
    small_q, small_k, small_v = (
        array.reshape(shares, STEPS, part_rows, HD).swapaxes(1, 2).reshape(rows, STEPS, HD)
        for array in project_small(
            later, table, by_chip(small_norm_gain[0]), small_projections[0],
            cosine, sine,
        )
    )
    small_heads = attend(
        small_q[:, :, None], small_cache[0, 0], small_cache[0, 1], small_k, small_v, lengths
    )
    small_heads = small_heads.reshape(shares, part_rows, STEPS, HD).swapaxes(1, 2)
    small_heads = small_heads.reshape(every_row, HD)

    sums = scatter_chips(
        mix(
            heads, swap_cores(heads), small_heads, table, core_index, base_output, output_other,
            small_output[0], width,
        )
    )
    base_gain = lax.dynamic_slice_in_dim(base_final_gain, block * width, width)
    small_gain = lax.dynamic_slice_in_dim(small_final_gain[0], chip * width, width)
    hidden = shard.astype(F32) + sums
    finals = gather_chips((hidden * jnp.concatenate([base_gain, small_gain])).astype(BF16))
    mine, theirs, squares = unembed_base(
        finals, table, core_index, 1.0 / half_of(base_final_gain), base_unembed, unembed_other,
    )
    later, _ = lax.optimization_barrier((finals, theirs))
    small_logits = unembed_small(
        later, table, core_index, 1.0 / by_chip(small_final_gain[0]),
        small_unembed[0].reshape(-1, small_unembed.shape[3]),
    )
    low, high = small_logits[:, :vocab_width], small_logits[:, vocab_width:]
    mean = (squares + swap_cores(squares))[:, :1] * (1.0 / features)
    steered = (mine + swap_cores(theirs)) * lax.rsqrt(mean + EPSILON)
    steered = steered + jnp.where(core == 0, low, high)
    steered = steered + swap_cores(jnp.where(core == 0, high, low))

    local_max = jnp.max(steered, axis=-1)
    local_sum = jnp.sum(jnp.exp(steered - local_max[:, None]), axis=-1)
    local_token = by_share(next_tokens) - block * vocab_width
    hit = jnp.arange(vocab_width)[None, :] == local_token[:, None]
    picked = jnp.sum(jnp.where(hit, steered, 0.0), axis=-1)
    triple = jnp.stack([local_max, local_sum, picked])
    count = lax.axis_size(EVERY)
    triples = lax.all_to_all(
        jnp.broadcast_to(triple[None], (count,) + triple.shape), EVERY, 0, 0, tiled=True
    )
    top = jnp.max(triples[:, 0], axis=0)
    total = jnp.sum(triples[:, 1] * jnp.exp(triples[:, 0] - top[None]), axis=0)
    log_norm = top + jnp.log(total)
    chosen = jnp.sum(triples[:, 2], axis=0) - log_norm
    log_probs = (steered - log_norm[:, None]).reshape(shares, STEPS, part_rows, vocab_width)
    log_probs = log_probs.swapaxes(0, 1).reshape(STEPS, rows, vocab_width)
    return log_probs, jnp.sum(chosen.reshape(shares, STEPS, part_rows), axis=1).reshape(rows)


def solution(mesh):
    devices = mesh.devices
    fine = Mesh(devices.reshape(2, 4, 2, 4, 2), ("grp", "z", "xl", "y", "dp"))
    placed = (
        P(None, "dp", EVERY),
        P("grp", None, "dp", CHIPS),
        P(),
        P(None, EVERY),
        P(None, None, EVERY),
        P(EVERY, None),
        P(None, "dp", EVERY, None),
        P(),
        P(EVERY, None),
        P("grp", None),
        P("grp", None, None, CHIPS),
        P("grp", CHIPS, None),
        P("grp", None, "dp", CHIPS, None),
        P("grp", None),
        P("grp", None, CHIPS, None),
        P("dp"),
        P(None, "dp"),
    )
    return jax.shard_map(
        body,
        mesh=fine,
        in_specs=placed,
        out_specs=(P(None, "dp", EVERY), P("dp")),
        check_vma=False,
    )
```
